128 devices in a mesh: ctx: 32 (over x, y, core), head: 4 (over z).
Axes of the slice: x: 4, y: 4, z: 4, core: 2. Of those that a mesh axis runs over, the one named last changes fastest.
Arguments:
- query: bfloat16 [4, 8192], P(None, 'head'), may hold values from -8 to 8
- key_cache: bfloat16 [4, 131072, 1024], P(None, 'ctx', 'head'), may hold values from -80 to 80
- cached_value_matrix: bfloat16 [4, 131072, 1024], P(None, 'ctx', 'head'), may hold values from -24 to 24
- lengths: int32 [4], replicated, may hold values from 2 to 131072, as said below
- out_weight: bfloat16 [8192, 8192], P('head', 'ctx'), may hold values from -0.0625 to 0.0625
Outputs:
- projected: float32 [4, 8192], P(None, 'ctx')
The draws below stay inside these ranges and needn't reach their ends.
Inputs may be any that keep to these rules, and one draw needn't show every extreme that they name: `lengths`: some sequence has exactly 131072 valid positions in every draw.
All inputs are finite; a program needn't handle non-finite values.
Results may differ from the reference program's by a relative error of at most 0.0095.
Values sent between devices are 32-bit elements; how exact they have to be, the bound alone decides.
No kernel may reach another device: no remote copies, remote signals or barrier semaphores. Data moves between devices by JAX's collectives and lax.ppermute only.
A program may use at most 64 MiB of HBM per device.

```python
import jax
import jax.numpy as jnp
from jax import lax

QUERY_HEADS = 64
KEY_VALUE_HEADS = 8
HEAD_WIDTH = 128
D = 8192
BATCH_ROWS = 4
CACHE_POSITIONS = 131072


def shared_queries(key):
    noise = jax.random.normal(key, (BATCH_ROWS, QUERY_HEADS * HEAD_WIDTH), jnp.float32)
    return jnp.clip(2.0 * noise, -8.0, 8.0)


def draw_query(key, part):
    base_offset = shared_queries(key)
    return base_offset.astype(jnp.bfloat16)


def draw_key_cache(key, part):
    key = jax.random.fold_in(key, 5)
    random_key = jax.random.fold_in(key, 0)
    key_block = jnp.clip(jax.random.normal(random_key, (BATCH_ROWS, CACHE_POSITIONS, KEY_VALUE_HEADS * HEAD_WIDTH), jnp.float32), -6.0, 6.0)
    return key_block.astype(jnp.bfloat16)


def draw_lengths(key, part):
    key = jax.random.fold_in(key, 7)
    length_key, pick_key = jax.random.split(key)
    drawn = jax.random.randint(length_key, (BATCH_ROWS,), 2, CACHE_POSITIONS, jnp.int32)
    chosen = jax.random.randint(pick_key, (), 0, BATCH_ROWS, jnp.int32)
    return jnp.where(jnp.arange(BATCH_ROWS, dtype=jnp.int32) == chosen, jnp.int32(CACHE_POSITIONS), drawn)


def shard_levels(stream_key, extent, cuts, smallest, high):
    gain = 1.0
    for dim, blocks in cuts:
        draws = jax.random.uniform(jax.random.fold_in(jax.random.fold_in(stream_key, 6), dim), (blocks,), jnp.float32, smallest / len(cuts), high / len(cuts))
        gain = gain * jnp.repeat(jnp.exp(draws), extent[dim] // blocks).reshape((-1,) + (1,) * (len(extent) - 1 - dim))
    return gain


def centred(rng, shape, deviation, most, cuts=(), kind=jnp.bfloat16):
    level = shard_levels(rng, shape, cuts, -0.22, 0.18) if cuts else 1.0
    result = jax.random.normal(rng, shape, jnp.float32) * deviation * level
    return jnp.minimum(jnp.maximum(result, -most), most).astype(kind)


def setup_inputs(seed: int = 0) -> dict:
    arg_keys = jax.random.split(jax.random.key(seed), 6)
    return {
        "query": draw_query(jax.random.fold_in(arg_keys[5], 71), 0),
        "key_cache": draw_key_cache(jax.random.fold_in(arg_keys[5], 71), 0),
        "cached_value_matrix": centred(arg_keys[2], (BATCH_ROWS, CACHE_POSITIONS, KEY_VALUE_HEADS * HEAD_WIDTH), 4.0, 24.0, ((1, 32), (2, 4))),
        "lengths": draw_lengths(jax.random.fold_in(arg_keys[5], 71), 0),
        "out_weight": centred(arg_keys[4], (QUERY_HEADS * HEAD_WIDTH, D), (QUERY_HEADS * HEAD_WIDTH) ** -0.5, 0.0625, ((0, 4), (1, 32))),
    }


def one_sequence(items):
    single_query_row, single_key_row, single_value_row, length = items
    query_group = QUERY_HEADS // KEY_VALUE_HEADS
    query_rows = single_query_row.astype(jnp.float32).reshape(KEY_VALUE_HEADS, query_group, HEAD_WIDTH)
    key_block = single_key_row.astype(jnp.float32).reshape(CACHE_POSITIONS, KEY_VALUE_HEADS, HEAD_WIDTH)
    value_block = single_value_row.astype(jnp.float32).reshape(CACHE_POSITIONS, KEY_VALUE_HEADS, HEAD_WIDTH)
    scores = jnp.einsum('gjd,cgd->gjc', query_rows, key_block) / jnp.sqrt(jnp.float32(HEAD_WIDTH))
    valid = (jnp.arange(CACHE_POSITIONS, dtype=jnp.int32) < length)[None, None, :]
    top = lax.optimization_barrier(jnp.max(jnp.where(valid, scores, jnp.float32(-1e+30)), axis=-1))
    weights = jnp.where(valid, jnp.exp(scores - top[..., None]), jnp.float32(0.0))
    total = lax.optimization_barrier(jnp.sum(weights, axis=-1))
    rounded = weights.astype(jnp.bfloat16).astype(jnp.float32)
    mixed = jnp.einsum('gjc,cgd->gjd', rounded, value_block)
    attended = (mixed / total[..., None]).astype(jnp.bfloat16)
    return attended.reshape(QUERY_HEADS * HEAD_WIDTH)

def reference(query, key_cache, cached_value_matrix, lengths, out_weight):
    attended = lax.map(one_sequence, (query, key_cache, cached_value_matrix, lengths.astype(jnp.int32)))
    return jnp.dot(attended, out_weight, preferred_element_type=jnp.float32)
```

```python
import functools

import jax
import jax.numpy as jnp
from jax import lax
from jax.experimental import pallas as pl
from jax.experimental.pallas import tpu as pltpu
from jax.sharding import PartitionSpec as P

HEAD_WIDTH = 128
LOWEST = -1e30
LOG2_E = 1.4426950408889634
PACKED = 72
MIB = 1 << 20


def attention_kernel(rows, heads, ctx_dev, lengths_hbm, query_hbm, key_hbm, value_hbm, out_ref,
                     lengths, query, query_rows, keys, values, scores, weights, small_sem, key_sem, value_sem):
    chunks = key_sem.shape[1]
    span = ctx_dev // chunks
    group = heads // 2

    def key_copy(r, c):
        piece = pl.ds(c * span, span)
        return pltpu.make_async_copy(key_hbm.at[r, piece], keys.at[r, piece], key_sem.at[r, c])

    def value_copy(r, c):
        piece = pl.ds(c * span, span)
        return pltpu.make_async_copy(value_hbm.at[r, piece], values.at[r, piece], value_sem.at[r, c])

    query_copy = pltpu.make_async_copy(query_hbm, query, small_sem.at[0])
    lengths_copy = pltpu.make_async_copy(lengths_hbm, lengths, small_sem.at[1])
    query_copy.start()
    lengths_copy.start()
    for r in range(rows):
        for c in range(chunks):
            key_copy(r, c).start()
    for r in range(rows):
        for c in range(chunks):
            value_copy(r, c).start()
    offset = lax.axis_index("ctx") * ctx_dev
    query_copy.wait()
    lengths_copy.wait()
    wide = query[...].astype(jnp.float32)
    for h in range(heads):
        query_rows[:, h, :] = wide[:, h * HEAD_WIDTH:(h + 1) * HEAD_WIDTH]
    nothing = jnp.zeros((group, HEAD_WIDTH), jnp.float32)
    tops, totals, mixes = [], [], []
    for r in range(rows):
        query_block = jnp.concatenate(
            [
                jnp.concatenate([query_rows[r, :group], nothing], axis=1),
                jnp.concatenate([nothing, query_rows[r, group:]], axis=1),
            ],
            axis=0,
        ).astype(jnp.bfloat16)
        place = offset + lax.broadcasted_iota(jnp.int32, (heads, span), 1)
        top = jnp.full((heads, 1), LOWEST, jnp.float32)
        for c in range(chunks):
            key_copy(r, c).wait()
            score = lax.dot_general(
                query_block, keys[r, c * span:(c + 1) * span], (((1,), (1,)), ((), ())),
                preferred_element_type=jnp.float32,
            ) * jnp.float32(LOG2_E / HEAD_WIDTH**0.5)
            score = jnp.where(place + c * span < lengths[r], score, jnp.float32(LOWEST))
            scores[:, c * span:(c + 1) * span] = score
            top = jnp.maximum(top, jnp.max(score, axis=1, keepdims=True))
        total = jnp.zeros((heads, 1), jnp.float32)
        for c in range(chunks):
            weight = jnp.where(
                place + c * span < lengths[r],
                jnp.exp2(scores[:, c * span:(c + 1) * span] - top),
                jnp.float32(0.0),
            )
            total += jnp.sum(weight, axis=1, keepdims=True)
            weights[r, :, c * span:(c + 1) * span] = weight.astype(jnp.bfloat16)
        tops.append(top)
        totals.append(total)
    for r in range(rows):
        mixed = jnp.zeros((heads, 2 * HEAD_WIDTH), jnp.float32)
        for c in range(chunks):
            value_copy(r, c).wait()
            mixed += jnp.dot(
                weights[r, :, c * span:(c + 1) * span], values[r, c * span:(c + 1) * span],
                preferred_element_type=jnp.float32,
            )
        mixes += [mixed[:group, :HEAD_WIDTH], mixed[group:, HEAD_WIDTH:]]
    lane = lax.broadcasted_iota(jnp.int32, (rows * heads, HEAD_WIDTH), 1)
    stats = jnp.where(lane == 0, jnp.concatenate(tops, axis=0), jnp.concatenate(totals, axis=0))
    turned = jnp.concatenate(mixes + mixes, axis=0).T
    half = rows * heads
    out_ref[:half] = jnp.where(lane < half, turned[:half], turned[half:])
    out_ref[half:] = jnp.concatenate([stats, stats], axis=0).T[:8]


def attention(query, key_cache, value_cache, lengths):
    rows, ctx_dev, kv_cols = key_cache.shape
    heads = query.shape[1] // HEAD_WIDTH
    chunks = 4
    hbm = pl.BlockSpec(memory_space=pl.ANY)
    return pl.pallas_call(
        functools.partial(attention_kernel, rows, heads, ctx_dev),
        out_shape=jax.ShapeDtypeStruct((PACKED, HEAD_WIDTH), jnp.float32),
        in_specs=[hbm] * 4,
        out_specs=pl.BlockSpec(memory_space=pltpu.VMEM),
        scratch_shapes=[
            pltpu.SMEM((rows,), jnp.int32),
            pltpu.VMEM(query.shape, jnp.bfloat16),
            pltpu.VMEM((rows, heads, HEAD_WIDTH), jnp.float32),
            pltpu.VMEM(key_cache.shape, jnp.bfloat16),
            pltpu.VMEM(value_cache.shape, jnp.bfloat16),
            pltpu.VMEM((heads, ctx_dev), jnp.float32),
            pltpu.VMEM((rows, heads, ctx_dev), jnp.bfloat16),
            pltpu.SemaphoreType.DMA((2,)),
            pltpu.SemaphoreType.DMA((rows, chunks)),
            pltpu.SemaphoreType.DMA((rows, chunks)),
        ],
        compiler_params=pltpu.CompilerParams(vmem_limit_bytes=32 * MIB),
        cost_estimate=pl.CostEstimate(
            flops=4 * rows * heads * ctx_dev * kv_cols, bytes_accessed=4 * rows * ctx_dev * kv_cols, transcendentals=0
        ),
    )(lengths, query, key_cache, value_cache)


def merge(pieces):
    half = PACKED - 8
    tops = [p[half:half + 1] for p in pieces]
    top = functools.reduce(jnp.maximum, tops)
    scales = [jnp.exp2(t - top) for t in tops]
    mixed = sum(p[:half] * s for p, s in zip(pieces, scales))
    total = sum(p[half + 1:half + 2] * s for p, s in zip(pieces, scales))
    return mixed, top, total


def merge_kernel(*refs):
    out_ref = refs[-1]
    mixed, top, total = merge([ref[...] for ref in refs[:-1]])
    half = mixed.shape[0]
    out_ref[:half] = mixed
    row = lax.broadcasted_iota(jnp.int32, (8, HEAD_WIDTH), 0)
    out_ref[half:] = jnp.where(row == 0, top, total)


def merge_call(pieces):
    vmem = pl.BlockSpec(memory_space=pltpu.VMEM)
    return pl.pallas_call(
        merge_kernel,
        out_shape=jax.ShapeDtypeStruct((PACKED, HEAD_WIDTH), jnp.float32),
        in_specs=[vmem] * len(pieces),
        out_specs=vmem,
    )(*pieces)


def project_kernel(rows, heads, *refs):
    *pieces, weight_ref, out_ref, attended = refs
    mixed, _, total = merge([ref[...] for ref in pieces])
    mixed = mixed / total
    half = mixed.shape[0]
    attended[...] = jnp.concatenate([mixed, pltpu.roll(mixed, half, 1)], axis=0).T[:half]
    flat = jnp.concatenate([attended[pl.ds(h, rows, stride=heads), :] for h in range(heads)], axis=1)
    out_ref[...] = jnp.dot(flat.astype(jnp.bfloat16), weight_ref[...], preferred_element_type=jnp.float32)


def project_call(pieces, out_weight, rows):
    heads = out_weight.shape[0] // HEAD_WIDTH
    vmem = pl.BlockSpec(memory_space=pltpu.VMEM)
    return pl.pallas_call(
        functools.partial(project_kernel, rows, heads),
        out_shape=jax.ShapeDtypeStruct((rows, out_weight.shape[1]), jnp.float32),
        in_specs=[vmem] * (len(pieces) + 1),
        out_specs=vmem,
        scratch_shapes=[pltpu.VMEM((rows * heads, HEAD_WIDTH), jnp.float32)],
        compiler_params=pltpu.CompilerParams(vmem_limit_bytes=16 * MIB),
    )(*pieces, out_weight)


def exchange(value, axis, bits):
    size = lax.axis_size(axis)
    return [value] + [lax.ppermute(value, axis, [(i, i ^ bit) for i in range(size)]) for bit in bits]


def on_device(query, key_cache, cached_value_matrix, lengths, out_weight):
    rows = query.shape[0]
    packed = attention(query, key_cache, cached_value_matrix, lengths)
    packed = merge_call(exchange(packed, "ctx", (1,)))
    packed = merge_call(exchange(packed, "ctx", (2, 6, 4)))
    partial_value = project_call(exchange(packed, "ctx", (8, 24, 16)), out_weight, rows)
    return functools.reduce(jnp.add, exchange(partial_value, "head", (1, 3, 2)))


def solution(mesh):
    in_specs = (
        P(None, "head"),
        P(None, "ctx", "head"),
        P(None, "ctx", "head"),
        P(),
        P("head", "ctx"),
    )
    out_specs = P(None, "ctx")
    return jax.shard_map(
        on_device, mesh=mesh, in_specs=in_specs, out_specs=out_specs, check_vma=False
    )
```

```python
import functools

import jax
import jax.numpy as jnp
from jax import lax
from jax.experimental import pallas as pl
from jax.experimental.pallas import tpu as pltpu
from jax.sharding import PartitionSpec as P

HEAD_WIDTH = 128
LOWEST = -1e30
LOG2_E = 1.4426950408889634
PACKED = 72
MIB = 1 << 20


def attention_kernel(per, ahead, lengths_hbm, query_hbm, key_hbm, value_hbm, out_ref,
                     lengths, query, query_rows, keys, values, scores, weights, small_sem, key_sem, value_sem):
    rows, ctx_dev, _ = keys.shape
    heads = query_rows.shape[1]
    group = heads // 2
    span = ctx_dev // per
    units = rows * per
    lag = 2

    def copy(unit, source, target, sem):
        r, c = divmod(unit, per)
        piece = pl.ds(c * span, span)
        return pltpu.make_async_copy(source.at[r, piece], target.at[r, piece], sem.at[unit])

    needs = [[] for _ in range(units + lag)]
    for unit in range(units):
        needs[unit].append(copy(unit, key_hbm, keys, key_sem))
        needs[unit + lag].append(copy(unit, value_hbm, values, value_sem))
    queue = [c for step in needs for c in step]
    query_copy = pltpu.make_async_copy(query_hbm, query, small_sem.at[0])
    lengths_copy = pltpu.make_async_copy(lengths_hbm, lengths, small_sem.at[1])
    query_copy.start()
    lengths_copy.start()
    for c in queue[:ahead]:
        c.start()
    started = min(ahead, len(queue))
    waited = 0

    offset = lax.axis_index("ctx") * ctx_dev
    query_copy.wait()
    lengths_copy.wait()
    wide = query[...].astype(jnp.float32)
    for h in range(heads):
        query_rows[:, h, :] = wide[:, h * HEAD_WIDTH:(h + 1) * HEAD_WIDTH]
    nothing = jnp.zeros((group, HEAD_WIDTH), jnp.float32)
    place = lax.broadcasted_iota(jnp.int32, (heads, span), 1)
    blocks, tops, totals, mixes = [], [], [], []
    for r in range(rows):
        blocks.append(
            jnp.concatenate(
                [
                    jnp.concatenate([query_rows[r, :group], nothing], axis=1),
                    jnp.concatenate([nothing, query_rows[r, group:]], axis=1),
                ],
                axis=0,
            ).astype(jnp.bfloat16)
        )
    for step in range(units + lag):
        for c in needs[step]:
            c.wait()
        waited += len(needs[step])
        for c in queue[started:waited + ahead]:
            c.start()
        started = max(started, min(waited + ahead, len(queue)))
        if step < units:
            r, c = divmod(step, per)
            scores[step % 2] = lax.dot_general(
                blocks[r], keys[r, c * span:(c + 1) * span], (((1,), (1,)), ((), ())),
                preferred_element_type=jnp.float32,
            )
        if 1 <= step <= units:
            r, c = divmod(step - 1, per)
            valid = place < lengths[r] - offset - c * span
            score = jnp.where(
                valid, scores[(step - 1) % 2] * jnp.float32(LOG2_E / HEAD_WIDTH**0.5), jnp.float32(LOWEST)
            )
            top = jnp.max(score, axis=1, keepdims=True)
            weight = jnp.where(valid, jnp.exp2(score - top), jnp.float32(0.0))
            tops.append(top)
            totals.append(jnp.sum(weight, axis=1, keepdims=True))
            weights[(step - 1) % 2] = weight.astype(jnp.bfloat16)
        if step >= lag:
            r, c = divmod(step - lag, per)
            both = jnp.dot(
                weights[step % 2], values[r, c * span:(c + 1) * span], preferred_element_type=jnp.float32
            )
            mixes.append(jnp.concatenate([both[:group, :HEAD_WIDTH], both[group:, HEAD_WIDTH:]], axis=0))
    row_mixes, row_tops, row_totals = [], [], []
    for r in range(rows):
        mine = slice(r * per, (r + 1) * per)
        top = functools.reduce(jnp.maximum, tops[mine])
        scales = [jnp.exp2(t - top) for t in tops[mine]]
        row_tops.append(top)
        row_totals.append(sum(t * s for t, s in zip(totals[mine], scales)))
        row_mixes.append(sum(m * s for m, s in zip(mixes[mine], scales)))
    lane = lax.broadcasted_iota(jnp.int32, (rows * heads, HEAD_WIDTH), 1)
    stats = jnp.where(lane == 0, jnp.concatenate(row_tops, axis=0), jnp.concatenate(row_totals, axis=0))
    turned = jnp.concatenate(row_mixes + row_mixes, axis=0).T
    half = rows * heads
    out_ref[:half] = jnp.where(lane < half, turned[:half], turned[half:])
    out_ref[half:] = jnp.concatenate([stats, stats], axis=0).T[:8]


def attention(query, key_cache, value_cache, lengths):
    rows, ctx_dev, kv_cols = key_cache.shape
    heads = query.shape[1] // HEAD_WIDTH
    per, ahead = 2, 8
    span = ctx_dev // per
    hbm = pl.BlockSpec(memory_space=pltpu.HBM)
    vmem = pl.BlockSpec(memory_space=pltpu.VMEM)
    return pl.pallas_call(
        functools.partial(attention_kernel, per, ahead),
        out_shape=jax.ShapeDtypeStruct((PACKED, HEAD_WIDTH), jnp.float32),
        in_specs=[hbm] * 4,
        out_specs=vmem,
        scratch_shapes=[
            pltpu.SMEM((rows,), jnp.int32),
            pltpu.VMEM(query.shape, jnp.bfloat16),
            pltpu.VMEM((rows, heads, HEAD_WIDTH), jnp.float32),
            pltpu.VMEM(key_cache.shape, jnp.bfloat16),
            pltpu.VMEM(value_cache.shape, jnp.bfloat16),
            pltpu.VMEM((2, heads, span), jnp.float32),
            pltpu.VMEM((2, heads, span), jnp.bfloat16),
            pltpu.SemaphoreType.DMA((2,)),
            pltpu.SemaphoreType.DMA((rows * per,)),
            pltpu.SemaphoreType.DMA((rows * per,)),
        ],
        compiler_params=pltpu.CompilerParams(vmem_limit_bytes=54 * MIB),
        cost_estimate=pl.CostEstimate(
            flops=4 * rows * heads * ctx_dev * kv_cols, bytes_accessed=4 * rows * ctx_dev * kv_cols, transcendentals=0
        ),
    )(lengths, query, key_cache, value_cache)


def fetch_kernel(source, target, sem):
    copy = pltpu.make_async_copy(source, target, sem)
    copy.start()
    copy.wait()


def fetch(packed):
    return pl.pallas_call(
        fetch_kernel,
        out_shape=jax.ShapeDtypeStruct(packed.shape, packed.dtype),
        in_specs=[pl.BlockSpec(memory_space=pltpu.HBM)],
        out_specs=pl.BlockSpec(memory_space=pltpu.VMEM),
        scratch_shapes=[pltpu.SemaphoreType.DMA],
        compiler_params=pltpu.CompilerParams(vmem_limit_bytes=4 * MIB),
        cost_estimate=pl.CostEstimate(flops=0, bytes_accessed=packed.size * 4, transcendentals=0),
    )(packed)


def merge(pieces):
    half = PACKED - 8
    tops = [p[half:half + 1] for p in pieces]
    top = functools.reduce(jnp.maximum, tops)
    scales = [jnp.exp2(t - top) for t in tops]
    mixed = sum(p[:half] * s for p, s in zip(pieces, scales))
    total = sum(p[half + 1:half + 2] * s for p, s in zip(pieces, scales))
    return mixed, top, total


def merge_kernel(*refs):
    out_ref = refs[-1]
    mixed, top, total = merge([ref[...] for ref in refs[:-1]])
    half = mixed.shape[0]
    out_ref[:half] = mixed
    row = lax.broadcasted_iota(jnp.int32, (8, HEAD_WIDTH), 0)
    out_ref[half:] = jnp.where(row == 0, top, total)


def merge_call(pieces):
    vmem = pl.BlockSpec(memory_space=pltpu.VMEM)
    return pl.pallas_call(
        merge_kernel,
        out_shape=jax.ShapeDtypeStruct((PACKED, HEAD_WIDTH), jnp.float32),
        in_specs=[vmem] * len(pieces),
        out_specs=vmem,
        compiler_params=pltpu.CompilerParams(vmem_limit_bytes=4 * MIB),
    )(*pieces)


def project_kernel(rows, heads, *refs):
    *pieces, weight_ref, out_ref, attended = refs
    mixed, _, total = merge([ref[...] for ref in pieces])
    mixed = mixed / total
    half = mixed.shape[0]
    attended[...] = jnp.concatenate([mixed, pltpu.roll(mixed, half, 1)], axis=0).T[:half]
    flat = jnp.concatenate([attended[pl.ds(h, rows, stride=heads), :] for h in range(heads)], axis=1)
    out_ref[...] = jnp.dot(flat.astype(jnp.bfloat16), weight_ref[...], preferred_element_type=jnp.float32)


def project_call(pieces, out_weight, rows):
    heads = out_weight.shape[0] // HEAD_WIDTH
    vmem = pl.BlockSpec(memory_space=pltpu.VMEM)
    return pl.pallas_call(
        functools.partial(project_kernel, rows, heads),
        out_shape=jax.ShapeDtypeStruct((rows, out_weight.shape[1]), jnp.float32),
        in_specs=[vmem] * (len(pieces) + 1),
        out_specs=vmem,
        scratch_shapes=[pltpu.VMEM((rows * heads, HEAD_WIDTH), jnp.float32)],
        compiler_params=pltpu.CompilerParams(vmem_limit_bytes=16 * MIB),
    )(*pieces, out_weight)


def exchange(value, axis, bits):
    size = lax.axis_size(axis)
    return [value] + [lax.ppermute(value, axis, [(i, i ^ bit) for i in range(size)]) for bit in bits]


def on_device(query, key_cache, cached_value_matrix, lengths, out_weight):
    rows = query.shape[0]
    packed = attention(query, key_cache, cached_value_matrix, lengths)
    packed = merge_call([fetch(packed)] + exchange(packed, "ctx", (1,))[1:])
    packed = merge_call(exchange(packed, "ctx", (2, 6, 4)))
    partial_value = project_call(exchange(packed, "ctx", (8, 24, 16)), out_weight, rows)
    return functools.reduce(jnp.add, exchange(partial_value, "head", (1, 3, 2)))


def solution(mesh):
    in_specs = (
        P(None, "head"),
        P(None, "ctx", "head"),
        P(None, "ctx", "head"),
        P(),
        P("head", "ctx"),
    )
    out_specs = P(None, "ctx")
    return jax.shard_map(
        on_device, mesh=mesh, in_specs=in_specs, out_specs=out_specs, check_vma=False
    )
```

```python
import functools

import jax
import jax.numpy as jnp
from jax import lax
from jax.experimental import pallas as pl
from jax.experimental.pallas import tpu as pltpu
from jax.sharding import PartitionSpec as P

HEAD_WIDTH = 128
LOWEST = -1e30
LOG2_E = 1.4426950408889634
PACKED = 72
MIB = 1 << 20


def attention_kernel(lengths_hbm, query_hbm, key_hbm, value_hbm, out_ref,
                     lengths, order, query, query_rows, blocks, keys, values, scores, weights, tops, totals, mixes,
                     small_sem, key_sem, value_sem):
    rows, ctx_dev, _ = keys.shape
    heads = query_rows.shape[1]
    group = heads // 2
    span = ctx_dev // 2

    def key_copy(r, c):
        piece = pl.ds(c * span, span)
        return pltpu.make_async_copy(key_hbm.at[r, piece], keys.at[r, piece], key_sem.at[r, c])

    def value_copy(r, c):
        piece = pl.ds(c * span, span)
        return pltpu.make_async_copy(value_hbm.at[r, piece], values.at[r, piece], value_sem.at[r, c])

    lengths_copy = pltpu.make_async_copy(lengths_hbm, lengths, small_sem.at[1])
    query_copy = pltpu.make_async_copy(query_hbm, query, small_sem.at[0])
    lengths_copy.start()
    query_copy.start()
    for c in range(2):
        key_copy(0, c).start()

    offset = lax.axis_index("ctx") * ctx_dev
    lengths_copy.wait()
    count = jnp.int32(0)
    for r in range(rows):
        order[count] = r
        count += (lengths[r] > offset).astype(jnp.int32)
    first_ready = lengths[0] > offset

    def start_keys(i, c):
        @pl.when(i < count)
        def _():
            key_copy(order[i], c).start()

    def start_values(i, c):
        @pl.when(i < count)
        def _():
            value_copy(order[i], c).start()

    @pl.when(jnp.logical_not(first_ready))
    def _():
        start_keys(0, 0)
        start_keys(0, 1)

    for c in range(2):
        start_keys(1, c)
        start_values(0, c)

    query_copy.wait()
    wide = query[...].astype(jnp.float32)
    for h in range(heads):
        query_rows[:, h, :] = wide[:, h * HEAD_WIDTH:(h + 1) * HEAD_WIDTH]
    nothing = jnp.zeros((group, HEAD_WIDTH), jnp.float32)
    for r in range(rows):
        blocks[r] = jnp.concatenate(
            [
                jnp.concatenate([query_rows[r, :group], nothing], axis=1),
                jnp.concatenate([nothing, query_rows[r, group:]], axis=1),
            ],
            axis=0,
        ).astype(jnp.bfloat16)
    tops[...] = jnp.full(tops.shape, LOWEST, jnp.float32)
    totals[...] = jnp.zeros(totals.shape, jnp.float32)
    mixes[...] = jnp.zeros(mixes.shape, jnp.float32)
    place = lax.broadcasted_iota(jnp.int32, (heads, span), 1)

    def score(r, c):
        scores[c] = lax.dot_general(
            blocks[r], keys[r, c * span:(c + 1) * span], (((1,), (1,)), ((), ())),
            preferred_element_type=jnp.float32,
        )

    def weigh(r, c):
        valid = place < lengths[r] - offset - c * span
        scaled = jnp.where(valid, scores[c] * jnp.float32(LOG2_E / HEAD_WIDTH**0.5), jnp.float32(LOWEST))
        top = jnp.max(scaled, axis=1, keepdims=True)
        weight = jnp.where(valid, jnp.exp2(scaled - top), jnp.float32(0.0))
        weights[c] = weight.astype(jnp.bfloat16)
        tops[r, c] = jnp.broadcast_to(top, (heads, HEAD_WIDTH))
        totals[r, c] = jnp.broadcast_to(jnp.sum(weight, axis=1, keepdims=True), (heads, HEAD_WIDTH))

    def mix(r, c):
        both = jnp.dot(weights[c], values[r, c * span:(c + 1) * span], preferred_element_type=jnp.float32)
        mixes[r, c] = jnp.concatenate([both[:group, :HEAD_WIDTH], both[group:, HEAD_WIDTH:]], axis=0)

    def go_on(i, c):
        start_keys(i + 2, c)
        start_values(i + 1, c)

    r = order[0]
    key_copy(r, 0).wait()
    go_on(0, 0)
    score(r, 0)
    key_copy(r, 1).wait()
    go_on(0, 1)
    score(r, 1)
    weigh(r, 0)

    def step(i, last):
        r = order[i]
        key_copy(r, 0).wait()
        value_copy(last, 0).wait()
        go_on(i, 0)
        mix(last, 0)
        weigh(last, 1)
        score(r, 0)
        key_copy(r, 1).wait()
        value_copy(last, 1).wait()
        go_on(i, 1)
        mix(last, 1)
        weigh(r, 0)
        score(r, 1)
        return r

    last = lax.fori_loop(1, count, step, r)
    value_copy(last, 0).wait()
    mix(last, 0)
    weigh(last, 1)
    value_copy(last, 1).wait()
    mix(last, 1)

    @pl.when(jnp.logical_not(first_ready))
    def _():
        for c in range(2):
            key_copy(0, c).wait()

    top = jnp.maximum(tops[:, 0], tops[:, 1])
    scales = [jnp.exp2(tops[:, c] - top) for c in range(2)]
    total = totals[:, 0] * scales[0] + totals[:, 1] * scales[1]
    mixed = mixes[:, 0] * scales[0] + mixes[:, 1] * scales[1]
    half = rows * heads
    top, total, mixed = (x.reshape(half, HEAD_WIDTH) for x in (top, total, mixed))
    lane = lax.broadcasted_iota(jnp.int32, (half, HEAD_WIDTH), 1)
    stats = jnp.where(lane == 0, top, total)
    turned = jnp.concatenate([mixed, mixed], axis=0).T
    out_ref[:half] = jnp.where(lane < half, turned[:half], turned[half:])
    out_ref[half:] = jnp.concatenate([stats, stats], axis=0).T[:8]


def attention(query, key_cache, value_cache, lengths):
    rows, ctx_dev, kv_cols = key_cache.shape
    heads = query.shape[1] // HEAD_WIDTH
    span = ctx_dev // 2
    hbm = pl.BlockSpec(memory_space=pltpu.HBM)
    return pl.pallas_call(
        attention_kernel,
        out_shape=jax.ShapeDtypeStruct((PACKED, HEAD_WIDTH), jnp.float32),
        in_specs=[hbm] * 4,
        out_specs=pl.BlockSpec(memory_space=pltpu.VMEM),
        scratch_shapes=[
            pltpu.SMEM((rows,), jnp.int32),
            pltpu.SMEM((rows + 1,), jnp.int32),
            pltpu.VMEM(query.shape, jnp.bfloat16),
            pltpu.VMEM((rows, heads, HEAD_WIDTH), jnp.float32),
            pltpu.VMEM((rows, heads, 2 * HEAD_WIDTH), jnp.bfloat16),
            pltpu.VMEM(key_cache.shape, jnp.bfloat16),
            pltpu.VMEM(value_cache.shape, jnp.bfloat16),
            pltpu.VMEM((2, heads, span), jnp.float32),
            pltpu.VMEM((2, heads, span), jnp.bfloat16),
            pltpu.VMEM((rows, 2, heads, HEAD_WIDTH), jnp.float32),
            pltpu.VMEM((rows, 2, heads, HEAD_WIDTH), jnp.float32),
            pltpu.VMEM((rows, 2, heads, HEAD_WIDTH), jnp.float32),
            pltpu.SemaphoreType.DMA((2,)),
            pltpu.SemaphoreType.DMA((rows, 2)),
            pltpu.SemaphoreType.DMA((rows, 2)),
        ],
        compiler_params=pltpu.CompilerParams(vmem_limit_bytes=54 * MIB),
        cost_estimate=pl.CostEstimate(
            flops=4 * rows * heads * ctx_dev * kv_cols, bytes_accessed=4 * rows * ctx_dev * kv_cols, transcendentals=0
        ),
    )(lengths, query, key_cache, value_cache)


def fetch_kernel(source, target, sem):
    copy = pltpu.make_async_copy(source, target, sem)
    copy.start()
    copy.wait()


def fetch(packed):
    return pl.pallas_call(
        fetch_kernel,
        out_shape=jax.ShapeDtypeStruct(packed.shape, packed.dtype),
        in_specs=[pl.BlockSpec(memory_space=pltpu.HBM)],
        out_specs=pl.BlockSpec(memory_space=pltpu.VMEM),
        scratch_shapes=[pltpu.SemaphoreType.DMA],
        compiler_params=pltpu.CompilerParams(vmem_limit_bytes=4 * MIB),
        cost_estimate=pl.CostEstimate(flops=0, bytes_accessed=packed.size * 4, transcendentals=0),
    )(packed)


def merge(pieces):
    half = PACKED - 8
    tops = [p[half:half + 1] for p in pieces]
    top = functools.reduce(jnp.maximum, tops)
    scales = [jnp.exp2(t - top) for t in tops]
    mixed = sum(p[:half] * s for p, s in zip(pieces, scales))
    total = sum(p[half + 1:half + 2] * s for p, s in zip(pieces, scales))
    return mixed, top, total


def merge_kernel(*refs):
    out_ref = refs[-1]
    mixed, top, total = merge([ref[...] for ref in refs[:-1]])
    half = mixed.shape[0]
    out_ref[:half] = mixed
    row = lax.broadcasted_iota(jnp.int32, (8, HEAD_WIDTH), 0)
    out_ref[half:] = jnp.where(row == 0, top, total)


def merge_call(pieces):
    vmem = pl.BlockSpec(memory_space=pltpu.VMEM)
    return pl.pallas_call(
        merge_kernel,
        out_shape=jax.ShapeDtypeStruct((PACKED, HEAD_WIDTH), jnp.float32),
        in_specs=[vmem] * len(pieces),
        out_specs=vmem,
        compiler_params=pltpu.CompilerParams(vmem_limit_bytes=4 * MIB),
    )(*pieces)


def project_kernel(rows, heads, *refs):
    *pieces, weight_ref, out_ref, attended = refs
    mixed, _, total = merge([ref[...] for ref in pieces])
    mixed = mixed / total
    half = mixed.shape[0]
    attended[...] = jnp.concatenate([mixed, pltpu.roll(mixed, half, 1)], axis=0).T[:half]
    flat = jnp.concatenate([attended[pl.ds(h, rows, stride=heads), :] for h in range(heads)], axis=1)
    out_ref[...] = jnp.dot(flat.astype(jnp.bfloat16), weight_ref[...], preferred_element_type=jnp.float32)


def project_call(pieces, out_weight, rows):
    heads = out_weight.shape[0] // HEAD_WIDTH
    vmem = pl.BlockSpec(memory_space=pltpu.VMEM)
    return pl.pallas_call(
        functools.partial(project_kernel, rows, heads),
        out_shape=jax.ShapeDtypeStruct((rows, out_weight.shape[1]), jnp.float32),
        in_specs=[vmem] * (len(pieces) + 1),
        out_specs=vmem,
        scratch_shapes=[pltpu.VMEM((rows * heads, HEAD_WIDTH), jnp.float32)],
        compiler_params=pltpu.CompilerParams(vmem_limit_bytes=16 * MIB),
    )(*pieces, out_weight)


def exchange(value, axis, bits):
    size = lax.axis_size(axis)
    return [value] + [lax.ppermute(value, axis, [(i, i ^ bit) for i in range(size)]) for bit in bits]


def on_device(query, key_cache, cached_value_matrix, lengths, out_weight):
    rows = query.shape[0]
    packed = attention(query, key_cache, cached_value_matrix, lengths)
    packed = merge_call([fetch(packed)] + exchange(packed, "ctx", (1,))[1:])
    packed = merge_call(exchange(packed, "ctx", (2, 6, 4)))
    partial_value = project_call(exchange(packed, "ctx", (8, 24, 16)), out_weight, rows)
    return functools.reduce(jnp.add, exchange(partial_value, "head", (1, 3, 2)))


def solution(mesh):
    in_specs = (
        P(None, "head"),
        P(None, "ctx", "head"),
        P(None, "ctx", "head"),
        P(),
        P("head", "ctx"),
    )
    out_specs = P(None, "ctx")
    return jax.shard_map(
        on_device, mesh=mesh, in_specs=in_specs, out_specs=out_specs, check_vma=False
    )
```

```python
import functools

import jax
import jax.numpy as jnp
from jax import lax
from jax.experimental import pallas as pl
from jax.experimental.pallas import tpu as pltpu
from jax.sharding import PartitionSpec as P

HEAD_WIDTH = 128
LOWEST = -1e30
LOG2_E = 1.4426950408889634
PACKED = 72
MIB = 1 << 20


def attention_kernel(lengths_hbm, query_hbm, key_hbm, value_hbm, out_ref,
                     lengths, order, query, query_rows, blocks, keys, values, scores, weights, tops, totals, mixes,
                     small_sem, key_sem, value_sem):
    rows, ctx_dev, _ = keys.shape
    heads = query_rows.shape[1]
    group = heads // 2
    span = ctx_dev // 2

    def key_copy(r, c):
        piece = pl.ds(c * span, span)
        return pltpu.make_async_copy(key_hbm.at[r, piece], keys.at[r, piece], key_sem.at[r, c])

    def value_copy(r, c):
        piece = pl.ds(c * span, span)
        return pltpu.make_async_copy(value_hbm.at[r, piece], values.at[r, piece], value_sem.at[r, c])

    lengths_copy = pltpu.make_async_copy(lengths_hbm, lengths, small_sem.at[1])
    query_copy = pltpu.make_async_copy(query_hbm, query, small_sem.at[0])
    lengths_copy.start()
    query_copy.start()
    for c in range(2):
        key_copy(0, c).start()

    offset = lax.axis_index("ctx") * ctx_dev
    lengths_copy.wait()
    count = jnp.int32(0)
    for r in range(rows):
        order[count] = r
        count += (lengths[r] > offset).astype(jnp.int32)
    first_ready = lengths[0] > offset

    def start_keys(i, c):
        @pl.when(i < count)
        def _():
            key_copy(order[i], c).start()

    def start_values(i, c):
        @pl.when(i < count)
        def _():
            value_copy(order[i], c).start()

    @pl.when(jnp.logical_not(first_ready))
    def _():
        start_keys(0, 0)
        start_keys(0, 1)

    for c in range(2):
        start_keys(1, c)
        start_values(0, c)

    query_copy.wait()
    wide = query[...].astype(jnp.float32)
    for h in range(heads):
        query_rows[:, h, :] = wide[:, h * HEAD_WIDTH:(h + 1) * HEAD_WIDTH]
    nothing = jnp.zeros((group, HEAD_WIDTH), jnp.float32)
    for r in range(rows):
        blocks[r] = jnp.concatenate(
            [
                jnp.concatenate([query_rows[r, :group], nothing], axis=1),
                jnp.concatenate([nothing, query_rows[r, group:]], axis=1),
            ],
            axis=0,
        ).astype(jnp.bfloat16)
    tops[...] = jnp.full(tops.shape, LOWEST, jnp.float32)
    totals[...] = jnp.zeros(totals.shape, jnp.float32)
    mixes[...] = jnp.zeros(mixes.shape, jnp.float32)
    place = lax.broadcasted_iota(jnp.int32, (heads, span), 1)

    def score(r, c):
        scores[c] = lax.dot_general(
            blocks[r], keys[r, c * span:(c + 1) * span], (((1,), (1,)), ((), ())),
            preferred_element_type=jnp.float32,
        )

    def weigh(r, c):
        valid = place < lengths[r] - offset - c * span
        scaled = jnp.where(valid, scores[c] * jnp.float32(LOG2_E / HEAD_WIDTH**0.5), jnp.float32(LOWEST))
        top = jnp.max(scaled, axis=1, keepdims=True)
        weight = jnp.where(valid, jnp.exp2(scaled - top), jnp.float32(0.0))
        weights[c] = weight.astype(jnp.bfloat16)
        tops[r, c] = jnp.broadcast_to(top, (heads, HEAD_WIDTH))
        totals[r, c] = jnp.broadcast_to(jnp.sum(weight, axis=1, keepdims=True), (heads, HEAD_WIDTH))

    def mix(r, c):
        both = jnp.dot(weights[c], values[r, c * span:(c + 1) * span], preferred_element_type=jnp.float32)
        mixes[r, c] = jnp.concatenate([both[:group, :HEAD_WIDTH], both[group:, HEAD_WIDTH:]], axis=0)

    def go_on(i, c):
        start_keys(i + 2, c)
        start_values(i + 1, c)

    r = order[0]
    key_copy(r, 0).wait()
    go_on(0, 0)
    score(r, 0)
    key_copy(r, 1).wait()
    go_on(0, 1)
    score(r, 1)
    weigh(r, 0)

    def step(i, last):
        r = order[i]
        key_copy(r, 0).wait()
        value_copy(last, 0).wait()
        go_on(i, 0)
        mix(last, 0)
        weigh(last, 1)
        score(r, 0)
        key_copy(r, 1).wait()
        value_copy(last, 1).wait()
        go_on(i, 1)
        mix(last, 1)
        weigh(r, 0)
        score(r, 1)
        return r

    last = lax.fori_loop(1, count, step, r)
    value_copy(last, 0).wait()
    mix(last, 0)
    weigh(last, 1)
    value_copy(last, 1).wait()
    mix(last, 1)

    @pl.when(jnp.logical_not(first_ready))
    def _():
        for c in range(2):
            key_copy(0, c).wait()

    top = jnp.maximum(tops[:, 0], tops[:, 1])
    scales = [jnp.exp2(tops[:, c] - top) for c in range(2)]
    total = totals[:, 0] * scales[0] + totals[:, 1] * scales[1]
    mixed = mixes[:, 0] * scales[0] + mixes[:, 1] * scales[1]
    half = rows * heads
    top, total, mixed = (x.reshape(half, HEAD_WIDTH) for x in (top, total, mixed))
    lane = lax.broadcasted_iota(jnp.int32, (half, HEAD_WIDTH), 1)
    stats = jnp.where(lane == 0, top, total)
    turned = jnp.concatenate([mixed, mixed], axis=0).T
    out_ref[:half] = jnp.where(lane < half, turned[:half], turned[half:])
    out_ref[half:] = jnp.concatenate([stats, stats], axis=0).T[:8]


def attention(query, key_cache, value_cache, lengths):
    rows, ctx_dev, kv_cols = key_cache.shape
    heads = query.shape[1] // HEAD_WIDTH
    span = ctx_dev // 2
    hbm = pl.BlockSpec(memory_space=pltpu.HBM)
    return pl.pallas_call(
        attention_kernel,
        out_shape=jax.ShapeDtypeStruct((PACKED, HEAD_WIDTH), jnp.float32),
        in_specs=[hbm] * 4,
        out_specs=pl.BlockSpec(memory_space=pltpu.VMEM),
        scratch_shapes=[
            pltpu.SMEM((rows,), jnp.int32),
            pltpu.SMEM((rows + 1,), jnp.int32),
            pltpu.VMEM(query.shape, jnp.bfloat16),
            pltpu.VMEM((rows, heads, HEAD_WIDTH), jnp.float32),
            pltpu.VMEM((rows, heads, 2 * HEAD_WIDTH), jnp.bfloat16),
            pltpu.VMEM(key_cache.shape, jnp.bfloat16),
            pltpu.VMEM(value_cache.shape, jnp.bfloat16),
            pltpu.VMEM((2, heads, span), jnp.float32),
            pltpu.VMEM((2, heads, span), jnp.bfloat16),
            pltpu.VMEM((rows, 2, heads, HEAD_WIDTH), jnp.float32),
            pltpu.VMEM((rows, 2, heads, HEAD_WIDTH), jnp.float32),
            pltpu.VMEM((rows, 2, heads, HEAD_WIDTH), jnp.float32),
            pltpu.SemaphoreType.DMA((2,)),
            pltpu.SemaphoreType.DMA((rows, 2)),
            pltpu.SemaphoreType.DMA((rows, 2)),
        ],
        compiler_params=pltpu.CompilerParams(vmem_limit_bytes=54 * MIB),
        cost_estimate=pl.CostEstimate(
            flops=4 * rows * heads * ctx_dev * kv_cols, bytes_accessed=4 * rows * ctx_dev * kv_cols, transcendentals=0
        ),
    )(lengths, query, key_cache, value_cache)


def fetch_kernel(source, target, sem):
    copy = pltpu.make_async_copy(source, target, sem)
    copy.start()
    copy.wait()


def fetch(packed):
    return pl.pallas_call(
        fetch_kernel,
        out_shape=jax.ShapeDtypeStruct(packed.shape, packed.dtype),
        in_specs=[pl.BlockSpec(memory_space=pltpu.HBM)],
        out_specs=pl.BlockSpec(memory_space=pltpu.VMEM),
        scratch_shapes=[pltpu.SemaphoreType.DMA],
        compiler_params=pltpu.CompilerParams(vmem_limit_bytes=4 * MIB),
        cost_estimate=pl.CostEstimate(flops=0, bytes_accessed=packed.size * 4, transcendentals=0),
    )(packed)


def merge(pieces):
    half = PACKED - 8
    tops = [p[half:half + 1] for p in pieces]
    top = functools.reduce(jnp.maximum, tops)
    scales = [jnp.exp2(t - top) for t in tops]
    mixed = sum(p[:half] * s for p, s in zip(pieces, scales))
    total = sum(p[half + 1:half + 2] * s for p, s in zip(pieces, scales))
    return mixed, top, total


def merge_kernel(*refs):
    out_ref = refs[-1]
    mixed, top, total = merge([ref[...] for ref in refs[:-1]])
    half = mixed.shape[0]
    out_ref[:half] = mixed
    row = lax.broadcasted_iota(jnp.int32, (8, HEAD_WIDTH), 0)
    out_ref[half:] = jnp.where(row == 0, top, total)


def merge_call(pieces):
    vmem = pl.BlockSpec(memory_space=pltpu.VMEM)
    return pl.pallas_call(
        merge_kernel,
        out_shape=jax.ShapeDtypeStruct((PACKED, HEAD_WIDTH), jnp.float32),
        in_specs=[vmem] * len(pieces),
        out_specs=vmem,
        compiler_params=pltpu.CompilerParams(vmem_limit_bytes=4 * MIB),
    )(*pieces)


def project_kernel(rows, heads, *refs):
    *pieces, weight_ref, out_ref, attended = refs
    mixed, _, total = merge([ref[...] for ref in pieces])
    mixed = mixed / total
    half = mixed.shape[0]
    attended[...] = jnp.concatenate([mixed, pltpu.roll(mixed, half, 1)], axis=0).T[:half]
    flat = jnp.concatenate([attended[pl.ds(h, rows, stride=heads), :] for h in range(heads)], axis=1)
    out_ref[...] = jnp.dot(flat.astype(jnp.bfloat16), weight_ref[...], preferred_element_type=jnp.float32)


def project_call(pieces, out_weight, rows):
    heads = out_weight.shape[0] // HEAD_WIDTH
    vmem = pl.BlockSpec(memory_space=pltpu.VMEM)
    return pl.pallas_call(
        functools.partial(project_kernel, rows, heads),
        out_shape=jax.ShapeDtypeStruct((rows, out_weight.shape[1]), jnp.float32),
        in_specs=[vmem] * (len(pieces) + 1),
        out_specs=vmem,
        scratch_shapes=[pltpu.VMEM((rows * heads, HEAD_WIDTH), jnp.float32)],
        compiler_params=pltpu.CompilerParams(vmem_limit_bytes=16 * MIB),
    )(*pieces, out_weight)


def exchange(value, axis, bits):
    size = lax.axis_size(axis)
    return [value] + [lax.ppermute(value, axis, [(i, i ^ bit) for i in range(size)]) for bit in bits]


def on_device(query, key_cache, cached_value_matrix, lengths, out_weight):
    rows = query.shape[0]
    packed = attention(query, key_cache, cached_value_matrix, lengths)
    packed = merge_call([fetch(packed)] + exchange(packed, "ctx", (1,))[1:])
    packed = merge_call(exchange(packed, "ctx", (3, 7, 5)))
    partial_value = project_call(exchange(packed, "ctx", (17, 25, 9)), out_weight, rows)
    return functools.reduce(jnp.add, exchange(partial_value, "head", (1, 3, 2)))


def solution(mesh):
    in_specs = (
        P(None, "head"),
        P(None, "ctx", "head"),
        P(None, "ctx", "head"),
        P(),
        P("head", "ctx"),
    )
    out_specs = P(None, "ctx")
    return jax.shard_map(
        on_device, mesh=mesh, in_specs=in_specs, out_specs=out_specs, check_vma=False
    )
```

```python
import functools

import jax
import jax.numpy as jnp
from jax import lax
from jax.experimental import pallas as pl
from jax.experimental.pallas import tpu as pltpu
from jax.sharding import PartitionSpec as P

HEAD_WIDTH = 128
LOWEST = -1e30
LOG2_E = 1.4426950408889634
PACKED = 72
MIB = 1 << 20


def attention_kernel(lengths_hbm, query_hbm, key_hbm, value_hbm, out_ref,
                     lengths, order, query, query_rows, blocks, keys, values, scores, weights, tops, totals, mixes,
                     small_sem, key_sem, value_sem):
    rows, ctx_dev, _ = keys.shape
    heads = query_rows.shape[1]
    group = heads // 2
    span = ctx_dev // 2

    def key_copy(r, c):
        piece = pl.ds(c * span, span)
        return pltpu.make_async_copy(key_hbm.at[r, piece], keys.at[r, piece], key_sem.at[r, c])

    def value_copy(r, c):
        piece = pl.ds(c * span, span)
        return pltpu.make_async_copy(value_hbm.at[r, piece], values.at[r, piece], value_sem.at[r, c])

    lengths_copy = pltpu.make_async_copy(lengths_hbm, lengths, small_sem.at[1])
    query_copy = pltpu.make_async_copy(query_hbm, query, small_sem.at[0])
    lengths_copy.start()
    query_copy.start()
    early = ((0, 0), (0, 1), (1, 0))
    for r, c in early:
        key_copy(r, c).start()

    offset = lax.axis_index("ctx") * ctx_dev
    lengths_copy.wait()
    count = jnp.int32(0)
    for r in range(rows):
        order[count] = r
        count += (lengths[r] > offset).astype(jnp.int32)

    def start_keys(i, c):
        r = order[i]
        started = r < 2 if c == 0 else r < 1

        @pl.when(jnp.logical_and(i < count, jnp.logical_not(started)))
        def _():
            key_copy(r, c).start()

    def start_values(i, c):
        @pl.when(i < count)
        def _():
            value_copy(order[i], c).start()

    start_keys(0, 0)
    start_keys(0, 1)
    for c in range(2):
        start_keys(1, c)
        start_values(0, c)

    query_copy.wait()
    wide = query[...].astype(jnp.float32)
    for h in range(heads):
        query_rows[:, h, :] = wide[:, h * HEAD_WIDTH:(h + 1) * HEAD_WIDTH]
    nothing = jnp.zeros((group, HEAD_WIDTH), jnp.float32)
    for r in range(rows):
        blocks[r] = jnp.concatenate(
            [
                jnp.concatenate([query_rows[r, :group], nothing], axis=1),
                jnp.concatenate([nothing, query_rows[r, group:]], axis=1),
            ],
            axis=0,
        ).astype(jnp.bfloat16)
    tops[...] = jnp.full(tops.shape, LOWEST, jnp.float32)
    totals[...] = jnp.zeros(totals.shape, jnp.float32)
    mixes[...] = jnp.zeros(mixes.shape, jnp.float32)
    place = lax.broadcasted_iota(jnp.int32, (heads, span), 1)

    def score(r, c):
        scores[c] = lax.dot_general(
            blocks[r], keys[r, c * span:(c + 1) * span], (((1,), (1,)), ((), ())),
            preferred_element_type=jnp.float32,
        )

    def weigh(r, c):
        valid = place < lengths[r] - offset - c * span
        scaled = jnp.where(valid, scores[c] * jnp.float32(LOG2_E / HEAD_WIDTH**0.5), jnp.float32(LOWEST))
        top = jnp.max(scaled, axis=1, keepdims=True)
        weight = jnp.where(valid, jnp.exp2(scaled - top), jnp.float32(0.0))
        weights[c] = weight.astype(jnp.bfloat16)
        tops[r, c] = jnp.broadcast_to(top, (heads, HEAD_WIDTH))
        totals[r, c] = jnp.broadcast_to(jnp.sum(weight, axis=1, keepdims=True), (heads, HEAD_WIDTH))

    def mix(r, c):
        both = jnp.dot(weights[c], values[r, c * span:(c + 1) * span], preferred_element_type=jnp.float32)
        mixes[r, c] = jnp.concatenate([both[:group, :HEAD_WIDTH], both[group:, HEAD_WIDTH:]], axis=0)

    def go_on(i, c):
        start_keys(i + 2, c)
        start_values(i + 1, c)

    r = order[0]
    key_copy(r, 0).wait()
    go_on(0, 0)
    score(r, 0)
    key_copy(r, 1).wait()
    go_on(0, 1)
    score(r, 1)
    weigh(r, 0)

    def step(i, last):
        r = order[i]
        key_copy(r, 0).wait()
        value_copy(last, 0).wait()
        go_on(i, 0)
        mix(last, 0)
        weigh(last, 1)
        score(r, 0)
        key_copy(r, 1).wait()
        value_copy(last, 1).wait()
        go_on(i, 1)
        mix(last, 1)
        weigh(r, 0)
        score(r, 1)
        return r

    last = lax.fori_loop(1, count, step, r)
    value_copy(last, 0).wait()
    mix(last, 0)
    weigh(last, 1)
    value_copy(last, 1).wait()
    mix(last, 1)

    for r, c in early:

        @pl.when(lengths[r] <= offset)
        def _(r=r, c=c):
            key_copy(r, c).wait()

    top = jnp.maximum(tops[:, 0], tops[:, 1])
    scales = [jnp.exp2(tops[:, c] - top) for c in range(2)]
    total = totals[:, 0] * scales[0] + totals[:, 1] * scales[1]
    mixed = mixes[:, 0] * scales[0] + mixes[:, 1] * scales[1]
    half = rows * heads
    top, total, mixed = (x.reshape(half, HEAD_WIDTH) for x in (top, total, mixed))
    lane = lax.broadcasted_iota(jnp.int32, (half, HEAD_WIDTH), 1)
    stats = jnp.where(lane == 0, top, total)
    turned = jnp.concatenate([mixed, mixed], axis=0).T
    out_ref[:half] = jnp.where(lane < half, turned[:half], turned[half:])
    out_ref[half:] = jnp.concatenate([stats, stats], axis=0).T[:8]


def attention(query, key_cache, value_cache, lengths):
    rows, ctx_dev, kv_cols = key_cache.shape
    heads = query.shape[1] // HEAD_WIDTH
    span = ctx_dev // 2
    hbm = pl.BlockSpec(memory_space=pltpu.HBM)
    return pl.pallas_call(
        attention_kernel,
        out_shape=jax.ShapeDtypeStruct((PACKED, HEAD_WIDTH), jnp.float32),
        in_specs=[hbm] * 4,
        out_specs=pl.BlockSpec(memory_space=pltpu.VMEM),
        scratch_shapes=[
            pltpu.SMEM((rows,), jnp.int32),
            pltpu.SMEM((rows + 1,), jnp.int32),
            pltpu.VMEM(query.shape, jnp.bfloat16),
            pltpu.VMEM((rows, heads, HEAD_WIDTH), jnp.float32),
            pltpu.VMEM((rows, heads, 2 * HEAD_WIDTH), jnp.bfloat16),
            pltpu.VMEM(key_cache.shape, jnp.bfloat16),
            pltpu.VMEM(value_cache.shape, jnp.bfloat16),
            pltpu.VMEM((2, heads, span), jnp.float32),
            pltpu.VMEM((2, heads, span), jnp.bfloat16),
            pltpu.VMEM((rows, 2, heads, HEAD_WIDTH), jnp.float32),
            pltpu.VMEM((rows, 2, heads, HEAD_WIDTH), jnp.float32),
            pltpu.VMEM((rows, 2, heads, HEAD_WIDTH), jnp.float32),
            pltpu.SemaphoreType.DMA((2,)),
            pltpu.SemaphoreType.DMA((rows, 2)),
            pltpu.SemaphoreType.DMA((rows, 2)),
        ],
        compiler_params=pltpu.CompilerParams(vmem_limit_bytes=54 * MIB),
        cost_estimate=pl.CostEstimate(
            flops=4 * rows * heads * ctx_dev * kv_cols, bytes_accessed=4 * rows * ctx_dev * kv_cols, transcendentals=0
        ),
    )(lengths, query, key_cache, value_cache)


def fetch_kernel(source, target, sem):
    copy = pltpu.make_async_copy(source, target, sem)
    copy.start()
    copy.wait()


def fetch(packed):
    return pl.pallas_call(
        fetch_kernel,
        out_shape=jax.ShapeDtypeStruct(packed.shape, packed.dtype),
        in_specs=[pl.BlockSpec(memory_space=pltpu.HBM)],
        out_specs=pl.BlockSpec(memory_space=pltpu.VMEM),
        scratch_shapes=[pltpu.SemaphoreType.DMA],
        compiler_params=pltpu.CompilerParams(vmem_limit_bytes=4 * MIB),
        cost_estimate=pl.CostEstimate(flops=0, bytes_accessed=packed.size * 4, transcendentals=0),
    )(packed)


def merge(pieces):
    half = PACKED - 8
    tops = [p[half:half + 1] for p in pieces]
    top = functools.reduce(jnp.maximum, tops)
    scales = [jnp.exp2(t - top) for t in tops]
    mixed = sum(p[:half] * s for p, s in zip(pieces, scales))
    total = sum(p[half + 1:half + 2] * s for p, s in zip(pieces, scales))
    return mixed, top, total


def merge_kernel(*refs):
    out_ref = refs[-1]
    mixed, top, total = merge([ref[...] for ref in refs[:-1]])
    half = mixed.shape[0]
    out_ref[:half] = mixed
    row = lax.broadcasted_iota(jnp.int32, (8, HEAD_WIDTH), 0)
    out_ref[half:] = jnp.where(row == 0, top, total)


def merge_call(pieces):
    vmem = pl.BlockSpec(memory_space=pltpu.VMEM)
    return pl.pallas_call(
        merge_kernel,
        out_shape=jax.ShapeDtypeStruct((PACKED, HEAD_WIDTH), jnp.float32),
        in_specs=[vmem] * len(pieces),
        out_specs=vmem,
        compiler_params=pltpu.CompilerParams(vmem_limit_bytes=4 * MIB),
    )(*pieces)


def project_kernel(rows, heads, *refs):
    *pieces, weight_ref, out_ref, attended = refs
    mixed, _, total = merge([ref[...] for ref in pieces])
    mixed = mixed / total
    half = mixed.shape[0]
    attended[...] = jnp.concatenate([mixed, pltpu.roll(mixed, half, 1)], axis=0).T[:half]
    flat = jnp.concatenate([attended[pl.ds(h, rows, stride=heads), :] for h in range(heads)], axis=1)
    out_ref[...] = jnp.dot(flat.astype(jnp.bfloat16), weight_ref[...], preferred_element_type=jnp.float32)


def project_call(pieces, out_weight, rows):
    heads = out_weight.shape[0] // HEAD_WIDTH
    vmem = pl.BlockSpec(memory_space=pltpu.VMEM)
    return pl.pallas_call(
        functools.partial(project_kernel, rows, heads),
        out_shape=jax.ShapeDtypeStruct((rows, out_weight.shape[1]), jnp.float32),
        in_specs=[vmem] * (len(pieces) + 1),
        out_specs=vmem,
        scratch_shapes=[pltpu.VMEM((rows * heads, HEAD_WIDTH), jnp.float32)],
        compiler_params=pltpu.CompilerParams(vmem_limit_bytes=16 * MIB),
    )(*pieces, out_weight)


def exchange(value, axis, perms):
    return [value] + [lax.ppermute(value, axis, perm) for perm in perms]


def along(axis, table):
    perm = []
    for x in range(4):
        for y in range(4):
            to_x, to_y = (table[x], y) if axis == "x" else (x, table[y])
            perm += [((x * 4 + y) * 2 + core, (to_x * 4 + to_y) * 2 + 1 - core) for core in range(2)]
    return perm


CORE = [[(i, i ^ 1) for i in range(32)]]
ALONG_Y = [along("y", table) for table in ((2, 0, 3, 1), (3, 2, 1, 0), (1, 3, 0, 2))]
ALONG_X = [along("x", table) for table in ((2, 3, 0, 1), (3, 2, 1, 0), (1, 0, 3, 2))]
ALONG_Z = [list(enumerate(table)) for table in ((2, 0, 3, 1), (3, 2, 1, 0), (1, 3, 0, 2))]


def on_device(query, key_cache, cached_value_matrix, lengths, out_weight):
    rows = query.shape[0]
    packed = attention(query, key_cache, cached_value_matrix, lengths)
    packed = merge_call([fetch(packed)] + exchange(packed, "ctx", CORE)[1:])
    packed = merge_call(exchange(packed, "ctx", ALONG_Y))
    partial_value = project_call(exchange(packed, "ctx", ALONG_X), out_weight, rows)
    return functools.reduce(jnp.add, exchange(partial_value, "head", ALONG_Z))


def solution(mesh):
    in_specs = (
        P(None, "head"),
        P(None, "ctx", "head"),
        P(None, "ctx", "head"),
        P(),
        P("head", "ctx"),
    )
    out_specs = P(None, "ctx")
    return jax.shard_map(
        on_device, mesh=mesh, in_specs=in_specs, out_specs=out_specs, check_vma=False
    )
```

```python
import functools

import jax
import jax.numpy as jnp
from jax import lax
from jax.experimental import pallas as pl
from jax.experimental.pallas import tpu as pltpu
from jax.sharding import PartitionSpec as P

HEAD_WIDTH = 128
LOWEST = -1e30
LOG2_E = 1.4426950408889634
PACKED = 72
MIB = 1 << 20


def attention_kernel(lengths_hbm, query_hbm, key_hbm, value_hbm, out_ref,
                     lengths, order, query, query_rows, blocks, keys, values, scores, weights, tops, totals, mixes,
                     small_sem, key_sem, value_sem):
    rows, ctx_dev, _ = keys.shape
    heads = query_rows.shape[1]
    group = heads // 2
    span = ctx_dev // 2

    def key_copy(r, c):
        piece = pl.ds(c * span, span)
        return pltpu.make_async_copy(key_hbm.at[r, piece], keys.at[r, piece], key_sem.at[r, c])

    def value_copy(r, c):
        piece = pl.ds(c * span, span)
        return pltpu.make_async_copy(value_hbm.at[r, piece], values.at[r, piece], value_sem.at[r, c])

    lengths_copy = pltpu.make_async_copy(lengths_hbm, lengths, small_sem.at[1])
    query_copy = pltpu.make_async_copy(query_hbm, query, small_sem.at[0])
    lengths_copy.start()
    query_copy.start()
    early = ((0, 0), (0, 1), (1, 0))
    for r, c in early:
        key_copy(r, c).start()

    offset = lax.axis_index("ctx") * ctx_dev
    lengths_copy.wait()
    count = jnp.int32(0)
    for r in range(rows):
        order[count] = r
        count += (lengths[r] > offset).astype(jnp.int32)

    def start_keys(i, c):
        @pl.when(i < count)
        def _():
            r = order[i]

            @pl.when(r >= (2 if c == 0 else 1))
            def _():
                key_copy(r, c).start()

    def start_values(i, c):
        @pl.when(i < count)
        def _():
            value_copy(order[i], c).start()

    start_keys(0, 0)
    start_keys(0, 1)
    for c in range(2):
        start_keys(1, c)
        start_values(0, c)

    query_copy.wait()
    wide = query[...].astype(jnp.float32)
    for h in range(heads):
        query_rows[:, h, :] = wide[:, h * HEAD_WIDTH:(h + 1) * HEAD_WIDTH]
    nothing = jnp.zeros((group, HEAD_WIDTH), jnp.float32)
    for r in range(rows):
        blocks[r] = jnp.concatenate(
            [
                jnp.concatenate([query_rows[r, :group], nothing], axis=1),
                jnp.concatenate([nothing, query_rows[r, group:]], axis=1),
            ],
            axis=0,
        ).astype(jnp.bfloat16)
    tops[...] = jnp.full(tops.shape, LOWEST, jnp.float32)
    totals[...] = jnp.zeros(totals.shape, jnp.float32)
    mixes[...] = jnp.zeros(mixes.shape, jnp.float32)
    place = lax.broadcasted_iota(jnp.int32, (heads, span), 1)

    def score(r, c):
        scores[c] = lax.dot_general(
            blocks[r], keys[r, c * span:(c + 1) * span], (((1,), (1,)), ((), ())),
            preferred_element_type=jnp.float32,
        )

    def weigh(r, c):
        valid = place < lengths[r] - offset - c * span
        scaled = jnp.where(valid, scores[c] * jnp.float32(LOG2_E / HEAD_WIDTH**0.5), jnp.float32(LOWEST))
        top = jnp.max(scaled, axis=1, keepdims=True)
        weight = jnp.where(valid, jnp.exp2(scaled - top), jnp.float32(0.0))
        weights[c] = weight.astype(jnp.bfloat16)
        tops[r, c] = jnp.broadcast_to(top, (heads, HEAD_WIDTH))
        totals[r, c] = jnp.broadcast_to(jnp.sum(weight, axis=1, keepdims=True), (heads, HEAD_WIDTH))

    def mix(r, c):
        both = jnp.dot(weights[c], values[r, c * span:(c + 1) * span], preferred_element_type=jnp.float32)
        mixes[r, c] = jnp.concatenate([both[:group, :HEAD_WIDTH], both[group:, HEAD_WIDTH:]], axis=0)

    def go_on(i, c):
        start_keys(i + 2, c)
        start_values(i + 1, c)

    r = order[0]
    key_copy(r, 0).wait()
    go_on(0, 0)
    score(r, 0)
    key_copy(r, 1).wait()
    go_on(0, 1)
    score(r, 1)
    weigh(r, 0)

    def step(i, last):
        r = order[i]
        key_copy(r, 0).wait()
        value_copy(last, 0).wait()
        go_on(i, 0)
        mix(last, 0)
        weigh(last, 1)
        score(r, 0)
        key_copy(r, 1).wait()
        value_copy(last, 1).wait()
        go_on(i, 1)
        mix(last, 1)
        weigh(r, 0)
        score(r, 1)
        return r

    last = lax.fori_loop(1, count, step, r)
    value_copy(last, 0).wait()
    mix(last, 0)
    weigh(last, 1)
    value_copy(last, 1).wait()
    mix(last, 1)

    for r, c in early:

        @pl.when(lengths[r] <= offset)
        def _(r=r, c=c):
            key_copy(r, c).wait()

    top = jnp.maximum(tops[:, 0], tops[:, 1])
    scales = [jnp.exp2(tops[:, c] - top) for c in range(2)]
    total = totals[:, 0] * scales[0] + totals[:, 1] * scales[1]
    mixed = mixes[:, 0] * scales[0] + mixes[:, 1] * scales[1]
    half = rows * heads
    top, total, mixed = (x.reshape(half, HEAD_WIDTH) for x in (top, total, mixed))
    lane = lax.broadcasted_iota(jnp.int32, (half, HEAD_WIDTH), 1)
    stats = jnp.where(lane == 0, top, total)
    turned = jnp.concatenate([mixed, mixed], axis=0).T
    out_ref[:half] = jnp.where(lane < half, turned[:half], turned[half:])
    out_ref[half:] = jnp.concatenate([stats, stats], axis=0).T[:8]


def attention(query, key_cache, value_cache, lengths):
    rows, ctx_dev, kv_cols = key_cache.shape
    heads = query.shape[1] // HEAD_WIDTH
    span = ctx_dev // 2
    hbm = pl.BlockSpec(memory_space=pltpu.HBM)
    return pl.pallas_call(
        attention_kernel,
        out_shape=jax.ShapeDtypeStruct((PACKED, HEAD_WIDTH), jnp.float32),
        in_specs=[hbm] * 4,
        out_specs=pl.BlockSpec(memory_space=pltpu.VMEM),
        scratch_shapes=[
            pltpu.SMEM((rows,), jnp.int32),
            pltpu.SMEM((rows + 1,), jnp.int32),
            pltpu.VMEM(query.shape, jnp.bfloat16),
            pltpu.VMEM((rows, heads, HEAD_WIDTH), jnp.float32),
            pltpu.VMEM((rows, heads, 2 * HEAD_WIDTH), jnp.bfloat16),
            pltpu.VMEM(key_cache.shape, jnp.bfloat16),
            pltpu.VMEM(value_cache.shape, jnp.bfloat16),
            pltpu.VMEM((2, heads, span), jnp.float32),
            pltpu.VMEM((2, heads, span), jnp.bfloat16),
            pltpu.VMEM((rows, 2, heads, HEAD_WIDTH), jnp.float32),
            pltpu.VMEM((rows, 2, heads, HEAD_WIDTH), jnp.float32),
            pltpu.VMEM((rows, 2, heads, HEAD_WIDTH), jnp.float32),
            pltpu.SemaphoreType.DMA((2,)),
            pltpu.SemaphoreType.DMA((rows, 2)),
            pltpu.SemaphoreType.DMA((rows, 2)),
        ],
        compiler_params=pltpu.CompilerParams(vmem_limit_bytes=54 * MIB),
        cost_estimate=pl.CostEstimate(
            flops=4 * rows * heads * ctx_dev * kv_cols, bytes_accessed=4 * rows * ctx_dev * kv_cols, transcendentals=0
        ),
    )(lengths, query, key_cache, value_cache)


def fetch_kernel(source, target, sem):
    copy = pltpu.make_async_copy(source, target, sem)
    copy.start()
    copy.wait()


def fetch(packed):
    return pl.pallas_call(
        fetch_kernel,
        out_shape=jax.ShapeDtypeStruct(packed.shape, packed.dtype),
        in_specs=[pl.BlockSpec(memory_space=pltpu.HBM)],
        out_specs=pl.BlockSpec(memory_space=pltpu.VMEM),
        scratch_shapes=[pltpu.SemaphoreType.DMA],
        compiler_params=pltpu.CompilerParams(vmem_limit_bytes=4 * MIB),
        cost_estimate=pl.CostEstimate(flops=0, bytes_accessed=packed.size * 4, transcendentals=0),
    )(packed)


def merge(pieces):
    half = PACKED - 8
    tops = [p[half:half + 1] for p in pieces]
    top = functools.reduce(jnp.maximum, tops)
    scales = [jnp.exp2(t - top) for t in tops]
    mixed = sum(p[:half] * s for p, s in zip(pieces, scales))
    total = sum(p[half + 1:half + 2] * s for p, s in zip(pieces, scales))
    return mixed, top, total


def merge_kernel(*refs):
    out_ref = refs[-1]
    mixed, top, total = merge([ref[...] for ref in refs[:-1]])
    half = mixed.shape[0]
    out_ref[:half] = mixed
    row = lax.broadcasted_iota(jnp.int32, (8, HEAD_WIDTH), 0)
    out_ref[half:] = jnp.where(row == 0, top, total)


def merge_call(pieces):
    vmem = pl.BlockSpec(memory_space=pltpu.VMEM)
    return pl.pallas_call(
        merge_kernel,
        out_shape=jax.ShapeDtypeStruct((PACKED, HEAD_WIDTH), jnp.float32),
        in_specs=[vmem] * len(pieces),
        out_specs=vmem,
        compiler_params=pltpu.CompilerParams(vmem_limit_bytes=4 * MIB),
    )(*pieces)


def project_kernel(rows, heads, *refs):
    *pieces, weight_ref, out_ref, attended = refs
    mixed, _, total = merge([ref[...] for ref in pieces])
    mixed = mixed / total
    half = mixed.shape[0]
    attended[...] = jnp.concatenate([mixed, pltpu.roll(mixed, half, 1)], axis=0).T[:half]
    flat = jnp.concatenate([attended[pl.ds(h, rows, stride=heads), :] for h in range(heads)], axis=1)
    out_ref[...] = jnp.dot(flat.astype(jnp.bfloat16), weight_ref[...], preferred_element_type=jnp.float32)


def project_call(pieces, out_weight, rows):
    heads = out_weight.shape[0] // HEAD_WIDTH
    vmem = pl.BlockSpec(memory_space=pltpu.VMEM)
    return pl.pallas_call(
        functools.partial(project_kernel, rows, heads),
        out_shape=jax.ShapeDtypeStruct((rows, out_weight.shape[1]), jnp.float32),
        in_specs=[vmem] * (len(pieces) + 1),
        out_specs=vmem,
        scratch_shapes=[pltpu.VMEM((rows * heads, HEAD_WIDTH), jnp.float32)],
        compiler_params=pltpu.CompilerParams(vmem_limit_bytes=16 * MIB),
    )(*pieces, out_weight)


def exchange(value, axis, perms):
    return [value] + [lax.ppermute(value, axis, perm) for perm in perms]


def along(axis, table):
    perm = []
    for x in range(4):
        for y in range(4):
            to_x, to_y = (table[x], y) if axis == "x" else (x, table[y])
            perm += [((x * 4 + y) * 2 + core, (to_x * 4 + to_y) * 2 + 1 - core) for core in range(2)]
    return perm


CORE = [[(i, i ^ 1) for i in range(32)]]
ALONG_Y = [along("y", table) for table in ((2, 0, 3, 1), (3, 2, 1, 0), (1, 3, 0, 2))]
ALONG_X = [along("x", table) for table in ((2, 3, 0, 1), (3, 2, 1, 0), (1, 0, 3, 2))]
ALONG_Z = [list(enumerate(table)) for table in ((2, 0, 3, 1), (3, 2, 1, 0), (1, 3, 0, 2))]


def on_device(query, key_cache, cached_value_matrix, lengths, out_weight):
    rows = query.shape[0]
    packed = attention(query, key_cache, cached_value_matrix, lengths)
    packed = merge_call([fetch(packed)] + exchange(packed, "ctx", CORE)[1:])
    packed = merge_call(exchange(packed, "ctx", ALONG_Y))
    partial_value = project_call(exchange(packed, "ctx", ALONG_X), out_weight, rows)
    return functools.reduce(jnp.add, exchange(partial_value, "head", ALONG_Z))


def solution(mesh):
    in_specs = (
        P(None, "head"),
        P(None, "ctx", "head"),
        P(None, "ctx", "head"),
        P(),
        P("head", "ctx"),
    )
    out_specs = P(None, "ctx")
    return jax.shard_map(
        on_device, mesh=mesh, in_specs=in_specs, out_specs=out_specs, check_vma=False
    )
```
